32 devices in a mesh: slab: 2 (over y), row: 4 (over z), col: 4 (over x, core).
Axes of the slice: x: 2, y: 2, z: 4, core: 2. Of those that a mesh axis runs over, the one named last changes fastest.
Arguments:
- inverse: bfloat16 [2, 8192, 4, 2048], P('slab', 'row', None, 'col'), may hold values from -0.0625 to 0.0625
- sources: bfloat16 [2, 4, 8192, 128], P('slab', None, ('row', 'col')), may hold values from -6 to 6
- coupling: float32 [2, 2, 8192], P('slab', None, ('row', 'col')), may hold values from -1 to 1
- plan: int32 [6, 2, 2], replicated, may hold values from 0 to 3
Outputs:
- up_out: bfloat16 [2, 8192, 128], P('slab', ('row', 'col'))
- down_out: bfloat16 [2, 8192, 128], P('slab', ('row', 'col'))
The draws below stay inside these ranges and needn't reach their ends.
Inputs may be any that keep to these rules, and one draw needn't show every extreme that they name: `plan`: each entry names one of the 4 stored batches of its slab.
All inputs are finite; a program needn't handle non-finite values.
Results may differ from the reference program's by a relative error of at most 0.023.
Values may be sent and summed in bfloat16 or wider, within the bound.
A program may use at most 64 MiB of HBM per device.

```python
import jax
import jax.numpy as jnp
from jax import lax

M = 8192
B = 128
TICKS = 6
NBATCH = 4
SLABS = 2
N_ROW = 4
N_COL = 4


def draw_coupling(key, part):
    base = jax.random.fold_in(key, 7331)
    sign_key, size_key = jax.random.split(base)
    sign_bits = jax.random.randint(sign_key, (SLABS, 2, M), 0, 2)
    signs = sign_bits.astype(jnp.float32) * 2.0 - 1.0
    lower = 0.9
    magnitude = jax.random.uniform(size_key, (SLABS, 2, M), jnp.float32, lower, 1.0)
    return (signs * magnitude).astype(jnp.float32)


def plant(values, rng, least, largest):
    extent = values.shape
    index_at = [jax.random.randint(jax.random.fold_in(rng, axis), (), 0, extent[axis]) for axis in range(len(extent))]
    values = values.at[tuple(index_at)].set(least)
    longest = extent.index(max(extent))
    index_at[longest] = (index_at[longest] + 1) % extent[longest]
    return values.at[tuple(index_at)].set(largest)


def shard_levels(stream_key, dims, pieces, least, top_value):
    loudness, own = 1.0, jax.random.fold_in(stream_key, 6)
    for position, parts in pieces:
        steps = jnp.exp(jax.random.uniform(jax.random.fold_in(own, position), (parts,), jnp.float32, least / len(pieces), top_value / len(pieces)))
        loudness = loudness * jnp.repeat(steps, dims[position] // parts).reshape([-1 if axis == position else 1 for axis in range(len(dims))])
    return loudness


def noise(rng, extent, width, bound, shards=(), kind=jnp.bfloat16):
    factor_of = shard_levels(rng, extent, shards, -0.22, 0.18) if shards else 1.0
    values = jax.random.normal(rng, extent, jnp.float32) * width * factor_of
    return jnp.minimum(jnp.maximum(values, -bound), bound).astype(kind)


def setup_inputs(seed: int = 0) -> dict:
    streams_of = jax.random.split(jax.random.key(seed), 5)
    inverse = noise(streams_of[0], (SLABS, M, N_ROW, M // N_ROW), M ** -0.5, 0.0625, ((0, 2), (1, 4), (3, 4)))
    sources = noise(streams_of[1], (SLABS, NBATCH, M, B), 1.0, 6.0, ((0, 2), (2, 16)))
    coupling = draw_coupling(jax.random.fold_in(streams_of[4], 71), 0)
    plan = plant(jax.random.randint(streams_of[3], (TICKS, SLABS, 2), 0, NBATCH), jax.random.fold_in(streams_of[3], 1), 0, NBATCH - 1).astype(jnp.int32)
    return dict(inverse=inverse, sources=sources, coupling=coupling, plan=plan)


def apply_up(matrix, vector):
    piece_rows = M // (N_ROW * N_COL)
    matrix_split = matrix.reshape(M, N_ROW, N_COL, piece_rows)
    vector_split = vector.reshape(N_ROW, N_COL, piece_rows, B)
    running = jnp.zeros((M, B), jnp.float32)
    for column_group in range(N_COL):
        columns = matrix_split[:, :, column_group, :].reshape(M, N_ROW * piece_rows)
        chosen = vector_split[:, column_group].reshape(N_ROW * piece_rows, B)
        partial_value = jnp.dot(columns, chosen, preferred_element_type=jnp.float32)
        rounded = lax.optimization_barrier(partial_value.astype(jnp.bfloat16))
        running = running + rounded.astype(jnp.float32)
    return running.astype(jnp.bfloat16)


def apply_down(matrix, vector):
    row_count = M // N_ROW
    running = jnp.zeros((M, B), jnp.float32)
    for row_group in range(N_ROW):
        row_block = matrix[row_group * row_count:(row_group + 1) * row_count]
        chosen = vector[row_group * row_count:(row_group + 1) * row_count]
        partial_value = lax.dot_general(row_block, chosen, (((0,), (0,)), ((), ())), preferred_element_type=jnp.float32)
        rounded = lax.optimization_barrier(partial_value.astype(jnp.bfloat16))
        running = running + rounded.astype(jnp.float32)
    return running.astype(jnp.bfloat16)


def reference(inverse, sources, coupling, plan):
    full = inverse.reshape(SLABS, M, M)
    up_out = jnp.zeros((SLABS, M, B), jnp.bfloat16)
    down_out = jnp.zeros((SLABS, M, B), jnp.bfloat16)
    slab_numbers = jnp.arange(SLABS, dtype=jnp.int32)
    zero_slab = jnp.zeros((1, M, B), jnp.bfloat16)
    for tick_index in range(TICKS):
        up_prev = jnp.concatenate([zero_slab, up_out[:-1]], axis=0)
        down_prev = jnp.concatenate([down_out[1:], zero_slab], axis=0)
        up_source = sources[slab_numbers, plan[tick_index, :, 0]]
        down_source = sources[slab_numbers, plan[tick_index, :, 1]]
        up_in = (up_source.astype(jnp.float32) + coupling[:, 0, :, None] * up_prev.astype(jnp.float32)).astype(jnp.bfloat16)
        down_in = (down_source.astype(jnp.float32) + coupling[:, 1, :, None] * down_prev.astype(jnp.float32)).astype(jnp.bfloat16)
        new_up = []
        new_down = []
        for slab_number in range(SLABS):
            new_up.append(apply_up(full[slab_number], up_in[slab_number]))
            new_down.append(apply_down(full[slab_number], down_in[slab_number]))
        up_out = jnp.stack(new_up)
        down_out = jnp.stack(new_down)
    return up_out, down_out
```

```python
import functools

import jax
import jax.numpy as jnp
from jax import lax
from jax.experimental import pallas as pl
from jax.experimental.pallas import tpu as pltpu
from jax.sharding import PartitionSpec as P

TICKS = 6
MESH = pl.DeviceIdType.MESH
f32 = jnp.float32
bf16 = jnp.bfloat16


def shifted(value, axis, steps):
    count = lax.axis_size(axis)
    leading, last = (max(0, -steps), min(count, count - steps))
    return lax.ppermute(value, axis, [(source, source + steps) for source in range(leading, last)])


def tick_by_tick(inverse, sources, coupling, plan):
    local_block = inverse[0]
    matrix = local_block.reshape(local_block.shape[0], -1)
    piece_rows, batch_width = sources.shape[2:]
    slab_index = lax.axis_index("slab")
    up_gain = coupling[0, 0][:, None]
    down_gain = coupling[0, 1][:, None]
    stored = sources[0]
    up_out = jnp.zeros((piece_rows, batch_width), bf16)
    down_out = jnp.zeros((piece_rows, batch_width), bf16)
    for tick in range(TICKS):
        up_recv, down_recv = up_out, down_out
        if tick:
            up_recv = shifted(up_out, "slab", 1)
            down_recv = shifted(down_out, "slab", -1)
        up_source = lax.dynamic_index_in_dim(stored, plan[tick, slab_index, 0], 0, keepdims=False)
        down_source = lax.dynamic_index_in_dim(stored, plan[tick, slab_index, 1], 0, keepdims=False)
        up_in = (up_source.astype(f32) + up_gain * up_recv.astype(f32)).astype(bf16)
        down_in = (down_source.astype(f32) + down_gain * down_recv.astype(f32)).astype(bf16)
        up_part = jnp.dot(matrix, lax.all_gather(up_in, "row", axis=0, tiled=True), preferred_element_type=f32)
        up_out = lax.psum_scatter(up_part.astype(bf16), "col", scatter_dimension=0, tiled=True)
        down_part = lax.dot_general(
            matrix,
            lax.all_gather(down_in, "col", axis=0, tiled=True),
            (((0,), (0,)), ((), ())),
            preferred_element_type=f32,
        )
        down_out = lax.psum_scatter(down_part.astype(bf16), "row", scatter_dimension=0, tiled=True)
    return (up_out[None], down_out[None])


def sweep_kernel(
    R, C, NB, T,
    plan, g, src, src_t, gain_up, gain_down,
    up_out, down_out,
    ux, up_part, up_got, up_first, up_second, up_in,
    dx, dn_part, dn_right, dn_left, dn_from_left, dn_from_right, dn_first, dn_second, dn_in,
    ux_s, ux_r, up_s, up_r, uy_s, uy_r,
    dx_s, dx_r, dr_s, dr_r, dl_s, dl_r, dy_s, dy_r,
):
    slab, r, c = lax.axis_index("slab"), lax.axis_index("row"), lax.axis_index("col")
    other = 1 - slab
    n, b = src.shape[1], src.shape[2]

    barrier = pltpu.get_barrier_semaphore()
    for step in (1, R - 1):
        pl.semaphore_signal(barrier, inc=1, device_id={"row": lax.rem(r + step, R)}, device_id_type=MESH)
    for step in range(1, C):
        pl.semaphore_signal(barrier, inc=1, device_id={"col": lax.rem(c + step, C)}, device_id_type=MESH)
    pl.semaphore_signal(barrier, inc=1, device_id={"slab": other}, device_id_type=MESH)
    pl.semaphore_wait(barrier, 2 + (C - 1) + 1)

    def remote(source, target, send, recv, **where):
        return pltpu.make_async_remote_copy(
            src_ref=source, dst_ref=target, send_sem=send, recv_sem=recv, device_id=where, device_id_type=MESH
        )

    def ux_copy(u, k, way):
        to = jnp.minimum(r + 1, R - 1) if way else jnp.maximum(r - 1, 0)
        return remote(ux.at[u, k], ux.at[u, k], ux_s.at[u, k, way], ux_r.at[u, k], row=to)

    def up_copy(u, to):
        return remote(up_part.at[u, to], up_got.at[u, c], up_s.at[u, to], up_r.at[u, c], col=to)

    def up_got_copy(u, origin):
        return remote(up_part.at[u, origin], up_got.at[u, origin], up_s.at[u, origin], up_r.at[u, origin], col=origin)

    def uy_copy(u):
        return remote(up_first.at[u], up_in.at[u], uy_s.at[u], uy_r.at[u], slab=other)

    def dx_copy(u, to):
        return remote(dx.at[u, c], dx.at[u, c], dx_s.at[u, to], dx_r.at[u, c], col=to)

    def dx_got_copy(u, origin):
        return remote(dx.at[u, origin], dx.at[u, origin], dx_s.at[u, origin], dx_r.at[u, origin], col=origin)

    def dr_copy(u, d):
        return remote(dn_right.at[u, d], dn_from_left.at[u, d], dr_s.at[u, d], dr_r.at[u, d], row=jnp.minimum(r + 1, R - 1))

    def dl_copy(u, d):
        return remote(dn_left.at[u, d], dn_from_right.at[u, d], dl_s.at[u, d], dl_r.at[u, d], row=jnp.maximum(r - 1, 0))

    def dy_copy(u):
        return remote(dn_first.at[u], dn_in.at[u], dy_s.at[u], dy_r.at[u], slab=other)

    def formed(source, gain, prev):
        return (source.astype(f32) + gain * prev.astype(f32)).astype(bf16)

    def up_form(phase, units):
        @pl.when(phase == 0)
        def _():
            @pl.loop(0, NB)
            def _(u):
                ux[u, r] = formed(src[u], gain_up[...], jnp.zeros((n, b), bf16))

        @pl.when(phase == 1)
        def _():
            @pl.loop(0, NB)
            def _(u):
                uy_copy(u).wait_recv()

            @pl.loop(0, T)
            def _(t):
                prev = up_in[plan[jnp.maximum(t - 1, 0), other, 0]].astype(f32)
                prev = jnp.where(t > 0, prev, 0.0)
                ux[t, r] = formed(src[plan[t, slab, 0]], gain_up[...], prev)

    def up_sweep(phase, units):
        up_form(phase, units)

        def own(u):
            @pl.when(r < R - 1)
            def _():
                ux_copy(u, r, 1).start()

            @pl.when(r > 0)
            def _():
                ux_copy(u, r, 0).start()

        own(0)
        own(1)

        @pl.loop(0, units + 1)
        def _(i):
            @pl.when(i < units)
            def _():
                for d in range(1, R):
                    @pl.when(r - d >= 0)
                    def _():
                        ux_copy(i, r - d, 1).wait_recv()

                        @pl.when(r < R - 1)
                        def _():
                            ux_copy(i, r - d, 1).start()

                    @pl.when(r + d < R)
                    def _():
                        ux_copy(i, r + d, 0).wait_recv()

                        @pl.when(r > 0)
                        def _():
                            ux_copy(i, r + d, 0).start()

                @pl.when(i + 2 < units)
                def _():
                    own(i + 2)

                @pl.loop(1, C + 1)
                def _(j):
                    to = lax.rem(c + j, C)
                    x = ux[i].reshape(R * n, b)
                    rows = pl.ds(pl.multiple_of(to * n, n), n)
                    up_part[i, to] = jnp.dot(g[rows, :], x, preferred_element_type=f32).astype(bf16)

                    @pl.when(j < C)
                    def _():
                        up_copy(i, to).start()

            @pl.when(i > 0)
            def _():
                u = i - 1
                total = up_part[u, c].astype(f32)
                for j in range(1, C):
                    origin = lax.rem(c + j, C)
                    up_got_copy(u, origin).wait_recv()
                    total = total + up_got[u, origin].astype(f32)

                @pl.when(phase == 0)
                def _():
                    up_first[u] = total.astype(bf16)
                    uy_copy(u).start()

                @pl.when(phase == 1)
                def _():
                    up_second[u] = total.astype(bf16)

    def up_drain(phase, units):
        @pl.loop(0, units)
        def _(u):
            for k in range(R):
                @pl.when(jnp.logical_and(r < R - 1, k <= r))
                def _():
                    ux_copy(u, k, 1).wait_send()

                @pl.when(jnp.logical_and(r > 0, k >= r))
                def _():
                    ux_copy(u, k, 0).wait_send()

            for j in range(1, C):
                up_copy(u, lax.rem(c + j, C)).wait_send()

            @pl.when(phase == 0)
            def _():
                uy_copy(u).wait_send()

    def down_form(phase, units):
        @pl.when(phase == 0)
        def _():
            @pl.loop(0, NB)
            def _(u):
                dx[u, c] = formed(src_t[u], gain_down[...], jnp.zeros((b, n), bf16))
                for j in range(1, C):
                    dx_copy(u, lax.rem(c + j, C)).start()

        @pl.when(phase == 1)
        def _():
            @pl.loop(0, NB)
            def _(u):
                dy_copy(u).wait_recv()

            @pl.loop(0, T)
            def _(t):
                prev = dn_in[plan[jnp.maximum(t - 1, 0), other, 1]].astype(f32)
                prev = jnp.where(t > 0, prev, 0.0)
                dx[t, c] = formed(src_t[plan[t, slab, 1]], gain_down[...], prev)
                for j in range(1, C):
                    dx_copy(t, lax.rem(c + j, C)).start()

    def down_sweep(phase, units):
        down_form(phase, units)

        @pl.loop(0, units + R - 1)
        def _(i):
            @pl.when(i < units)
            def _():
                for j in range(1, C):
                    dx_got_copy(i, lax.rem(c + j, C)).wait_recv()

                @pl.loop(0, R)
                def _(k):
                    cols = pl.ds(pl.multiple_of(k * n, n), n)
                    total = jnp.dot(dx[i, 0], g[0:n, cols], preferred_element_type=f32)
                    for q in range(1, C):
                        total += jnp.dot(dx[i, q], g[q * n:(q + 1) * n, cols], preferred_element_type=f32)
                    dn_part[i, k] = total.astype(bf16)

            ur = i - r

            @pl.when(jnp.logical_and(r < R - 1, jnp.logical_and(ur >= 0, ur < units)))
            def _():
                for d in reversed(range(1, R)):
                    @pl.when(d > r)
                    def _():
                        @pl.when(r == 0)
                        def _():
                            dn_right[ur, d] = dn_part[ur, d]

                        @pl.when(r > 0)
                        def _():
                            dr_copy(ur, d).wait_recv()
                            dn_right[ur, d] = (dn_part[ur, d].astype(f32) + dn_from_left[ur, d].astype(f32)).astype(bf16)

                        dr_copy(ur, d).start()

            ul = i - (R - 1 - r)

            @pl.when(jnp.logical_and(r > 0, jnp.logical_and(ul >= 0, ul < units)))
            def _():
                for d in range(R - 1):
                    @pl.when(d < r)
                    def _():
                        @pl.when(r == R - 1)
                        def _():
                            dn_left[ul, d] = dn_part[ul, d]

                        @pl.when(r < R - 1)
                        def _():
                            dl_copy(ul, d).wait_recv()
                            dn_left[ul, d] = (dn_part[ul, d].astype(f32) + dn_from_right[ul, d].astype(f32)).astype(bf16)

                        dl_copy(ul, d).start()

            @pl.when(i >= R - 1)
            def _():
                u = i - (R - 1)

                def finish(total):
                    @pl.when(phase == 0)
                    def _():
                        dn_first[u] = total.astype(bf16)
                        dy_copy(u).start()

                    @pl.when(phase == 1)
                    def _():
                        dn_second[u] = total.astype(bf16)

                @pl.when(r > 0)
                def _():
                    dr_copy(u, r).wait_recv()

                @pl.when(r < R - 1)
                def _():
                    dl_copy(u, r).wait_recv()

                mine = dn_part[u, r].astype(f32)

                @pl.when(r == 0)
                def _():
                    finish(mine + dn_from_right[u, r].astype(f32))

                @pl.when(r == R - 1)
                def _():
                    finish(mine + dn_from_left[u, r].astype(f32))

                @pl.when(jnp.logical_and(r > 0, r < R - 1))
                def _():
                    finish(mine + dn_from_left[u, r].astype(f32) + dn_from_right[u, r].astype(f32))

    def down_drain(phase, units):
        @pl.loop(0, units)
        def _(u):
            for j in range(1, C):
                dx_copy(u, lax.rem(c + j, C)).wait_send()
            for d in range(R):
                @pl.when(d > r)
                def _():
                    dr_copy(u, d).wait_send()

                @pl.when(d < r)
                def _():
                    dl_copy(u, d).wait_send()

            @pl.when(phase == 0)
            def _():
                dy_copy(u).wait_send()

    @pl.loop(0, 2)
    def _(phase):
        units = jnp.where(phase == 0, NB, T)
        upward = lax.rem(phase + slab, 2) == 0

        @pl.when(upward)
        def _():
            up_sweep(phase, units)
            up_drain(phase, units)

        @pl.when(jnp.logical_not(upward))
        def _():
            down_sweep(phase, units)
            down_drain(phase, units)

    @pl.when(slab == 0)
    def _():
        up_out[...] = up_first[plan[T - 1, slab, 0]]
        down_out[...] = dn_second[T - 1]

    @pl.when(slab == 1)
    def _():
        up_out[...] = up_second[T - 1]
        down_out[...] = dn_first[plan[T - 1, slab, 1]]


def two_slabs(R, C, inverse, sources, coupling, plan):
    matrix = inverse[0].reshape(inverse.shape[1], -1)
    src = sources[0]
    NB, n, b = src.shape
    T = TICKS
    V = lambda *shape: pltpu.VMEM(shape, bf16)
    D = lambda *shape: pltpu.SemaphoreType.DMA(shape)
    vmem = pl.BlockSpec(memory_space=pltpu.VMEM)
    flops = 2 * matrix.size * b * (NB + T)
    up, down_t = pl.pallas_call(
        functools.partial(sweep_kernel, R, C, NB, T),
        out_shape=(jax.ShapeDtypeStruct((n, b), bf16), jax.ShapeDtypeStruct((b, n), bf16)),
        in_specs=[pl.BlockSpec(memory_space=pltpu.SMEM)] + [vmem] * 5,
        out_specs=(vmem, vmem),
        scratch_shapes=[
            V(T, R, n, b), V(T, C, n, b), V(T, C, n, b), V(NB, n, b), V(T, n, b), V(NB, n, b),
            V(T, C, b, n), V(T, R, b, n), V(T, R, b, n), V(T, R, b, n), V(T, R, b, n), V(T, R, b, n),
            V(NB, b, n), V(T, b, n), V(NB, b, n),
            D(T, R, 2), D(T, R), D(T, C), D(T, C), D(NB), D(NB),
            D(T, C), D(T, C), D(T, R), D(T, R), D(T, R), D(T, R), D(NB), D(NB),
        ],
        compiler_params=pltpu.CompilerParams(
            collective_id=0, has_side_effects=True, vmem_limit_bytes=56 * 1024 * 1024
        ),
        cost_estimate=pl.CostEstimate(flops=flops, bytes_accessed=2 * matrix.size, transcendentals=0),
    )(
        plan, matrix, src, jnp.swapaxes(src, 1, 2), coupling[0, 0][:, None], coupling[0, 1][None, :],
    )
    return up[None], down_t.T[None]


def solution(mesh):
    placed = (
        P("slab", "row", None, "col"),
        P("slab", None, ("row", "col"), None),
        P("slab", None, ("row", "col")),
        P(),
    )
    sizes = mesh.shape
    body = tick_by_tick
    if sizes["slab"] == 2 and sizes["row"] > 2 and sizes["col"] > 1:
        body = functools.partial(two_slabs, sizes["row"], sizes["col"])
    return jax.shard_map(
        body,
        mesh=mesh,
        in_specs=placed,
        out_specs=(P("slab", ("row", "col"), None), P("slab", ("row", "col"), None)),
        check_vma=False,
    )
```

```python
import functools

import jax
import jax.numpy as jnp
from jax import lax
from jax.experimental import pallas as pl
from jax.experimental.pallas import tpu as pltpu
from jax.sharding import PartitionSpec as P

TICKS = 6
MESH = pl.DeviceIdType.MESH
f32 = jnp.float32
bf16 = jnp.bfloat16


def shifted(value, axis, steps):
    count = lax.axis_size(axis)
    leading, last = (max(0, -steps), min(count, count - steps))
    return lax.ppermute(value, axis, [(source, source + steps) for source in range(leading, last)])


def tick_by_tick(inverse, sources, coupling, plan):
    local_block = inverse[0]
    matrix = local_block.reshape(local_block.shape[0], -1)
    piece_rows, batch_width = sources.shape[2:]
    slab_index = lax.axis_index("slab")
    up_gain = coupling[0, 0][:, None]
    down_gain = coupling[0, 1][:, None]
    stored = sources[0]
    up_out = jnp.zeros((piece_rows, batch_width), bf16)
    down_out = jnp.zeros((piece_rows, batch_width), bf16)
    for tick in range(TICKS):
        up_recv, down_recv = up_out, down_out
        if tick:
            up_recv = shifted(up_out, "slab", 1)
            down_recv = shifted(down_out, "slab", -1)
        up_source = lax.dynamic_index_in_dim(stored, plan[tick, slab_index, 0], 0, keepdims=False)
        down_source = lax.dynamic_index_in_dim(stored, plan[tick, slab_index, 1], 0, keepdims=False)
        up_in = (up_source.astype(f32) + up_gain * up_recv.astype(f32)).astype(bf16)
        down_in = (down_source.astype(f32) + down_gain * down_recv.astype(f32)).astype(bf16)
        up_part = jnp.dot(matrix, lax.all_gather(up_in, "row", axis=0, tiled=True), preferred_element_type=f32)
        up_out = lax.psum_scatter(up_part.astype(bf16), "col", scatter_dimension=0, tiled=True)
        down_part = lax.dot_general(
            matrix,
            lax.all_gather(down_in, "col", axis=0, tiled=True),
            (((0,), (0,)), ((), ())),
            preferred_element_type=f32,
        )
        down_out = lax.psum_scatter(down_part.astype(bf16), "row", scatter_dimension=0, tiled=True)
    return (up_out[None], down_out[None])


def sweep_kernel(
    R, C, NB, T,
    plan, g, src, src_t, gain_up, gain_down,
    up_out, down_out,
    ux, up_part, up_got, up_mid, up_first, up_second, up_in,
    dx, dn_part, dn_right, dn_left, dn_from_left, dn_from_right, dn_first, dn_second, dn_in,
    ux_s, ux_r, up_s, up_r, uy_s, uy_r,
    dx_s, dx_r, dr_s, dr_r, dl_s, dl_r, dy_s, dy_r,
    mid_s, mid_r, pass_s,
):
    slab, r, c = lax.axis_index("slab"), lax.axis_index("row"), lax.axis_index("col")
    other = 1 - slab
    n, b = src.shape[1], src.shape[2]
    sib = c + 1 - 2 * lax.rem(c, 2)
    far = [lax.rem(c + j, C) for j in range(2, C, 2)]

    barrier = pltpu.get_barrier_semaphore()
    for step in (1, R - 1):
        pl.semaphore_signal(barrier, inc=1, device_id={"row": lax.rem(r + step, R)}, device_id_type=MESH)
    for step in range(1, C):
        pl.semaphore_signal(barrier, inc=1, device_id={"col": lax.rem(c + step, C)}, device_id_type=MESH)
    pl.semaphore_signal(barrier, inc=1, device_id={"slab": other}, device_id_type=MESH)
    pl.semaphore_wait(barrier, 2 + (C - 1) + 1)

    def remote(source, target, send, recv, **where):
        return pltpu.make_async_remote_copy(
            src_ref=source, dst_ref=target, send_sem=send, recv_sem=recv, device_id=where, device_id_type=MESH
        )

    def ux_copy(u, k, way):
        to = jnp.minimum(r + 1, R - 1) if way else jnp.maximum(r - 1, 0)
        return remote(ux.at[u, k], ux.at[u, k], ux_s.at[u, k, way], ux_r.at[u, k], row=to)

    def up_copy(u, to):
        return remote(up_part.at[u, to], up_got.at[u, c], up_s.at[u, to], up_r.at[u, c], col=to)

    def up_got_copy(u, origin):
        return remote(up_part.at[u, origin], up_got.at[u, origin], up_s.at[u, origin], up_r.at[u, origin], col=origin)

    def mid_copy(u, dest):
        return remote(up_part.at[u, dest], up_mid.at[u, dest], mid_s.at[u, dest], mid_r.at[u, dest], col=sib)

    def uy_copy(u):
        return remote(up_first.at[u], up_in.at[u], uy_s.at[u], uy_r.at[u], slab=other)

    def dx_copy(u, to):
        return remote(dx.at[u, c], dx.at[u, c], dx_s.at[u, to], dx_r.at[u, c], col=to)

    def pass_copy(u, origin):
        return remote(dx.at[u, origin], dx.at[u, origin], pass_s.at[u, origin], dx_r.at[u, origin], col=sib)

    def dx_got_copy(u, origin):
        return remote(dx.at[u, origin], dx.at[u, origin], dx_s.at[u, origin], dx_r.at[u, origin], col=origin)

    def dr_copy(u, d):
        return remote(dn_right.at[u, d], dn_from_left.at[u, d], dr_s.at[u, d], dr_r.at[u, d], row=jnp.minimum(r + 1, R - 1))

    def dl_copy(u, d):
        return remote(dn_left.at[u, d], dn_from_right.at[u, d], dl_s.at[u, d], dl_r.at[u, d], row=jnp.maximum(r - 1, 0))

    def dy_copy(u):
        return remote(dn_first.at[u], dn_in.at[u], dy_s.at[u], dy_r.at[u], slab=other)

    def formed(source, gain, prev):
        return (source.astype(f32) + gain * prev.astype(f32)).astype(bf16)

    def up_form(phase, units):
        @pl.when(phase == 0)
        def _():
            @pl.loop(0, NB)
            def _(u):
                ux[u, r] = formed(src[u], gain_up[...], jnp.zeros((n, b), bf16))

        @pl.when(phase == 1)
        def _():
            @pl.loop(0, NB)
            def _(u):
                uy_copy(u).wait_recv()

            @pl.loop(1, T)
            def _(t):
                prev = up_in[plan[t - 1, other, 0]]
                ux[t, r] = formed(src[plan[t, slab, 0]], gain_up[...], prev)

    def own(u):
        @pl.when(r < R - 1)
        def _():
            ux_copy(u, r, 1).start()

        @pl.when(r > 0)
        def _():
            ux_copy(u, r, 0).start()

    def up_sweep(phase, units):
        up_form(phase, units)

        @pl.when(phase == 0)
        def _():
            own(0)

        @pl.loop(0, units + R - 1)
        def _(i):
            @pl.when(i + 1 < units)
            def _():
                own(i + 1)

            for d in reversed(range(1, R)):
                u = i - (d - 1)

                @pl.when(jnp.logical_and(u >= 0, u < units))
                def _():
                    @pl.when(r - d >= 0)
                    def _():
                        ux_copy(u, r - d, 1).wait_recv()

                        @pl.when(r < R - 1)
                        def _():
                            ux_copy(u, r - d, 1).start()

                    @pl.when(r + d < R)
                    def _():
                        ux_copy(u, r + d, 0).wait_recv()

                        @pl.when(r > 0)
                        def _():
                            ux_copy(u, r + d, 0).start()

            um = i - (R - 2)

            @pl.when(jnp.logical_and(um >= 0, um < units))
            def _():
                @pl.loop(1, C // 2 + 1)
                def _(j):
                    to = lax.rem(sib + 2 * j, C)
                    rows = pl.ds(pl.multiple_of(to * n, n), n)
                    x = ux[um].reshape(R * n, b)
                    up_part[um, to] = jnp.dot(g[rows, :], x, preferred_element_type=f32).astype(bf16)

                    @pl.when(j < C // 2)
                    def _():
                        mid_copy(um, to).start()

                    @pl.when(j == C // 2)
                    def _():
                        up_copy(um, sib).start()

                @pl.loop(1, C // 2 + 1)
                def _(j):
                    to = lax.rem(c + 2 * j, C)
                    rows = pl.ds(pl.multiple_of(to * n, n), n)
                    x = ux[um].reshape(R * n, b)
                    up_part[um, to] = jnp.dot(g[rows, :], x, preferred_element_type=f32).astype(bf16)

                    @pl.when(j < C // 2)
                    def _():
                        mid_copy(um, to).wait_recv()
                        up_part[um, to] = (up_part[um, to].astype(f32) + up_mid[um, to].astype(f32)).astype(bf16)
                        up_copy(um, to).start()

            @pl.when(i >= R - 1)
            def _():
                u = i - (R - 1)
                total = up_part[u, c].astype(f32)
                for origin in [sib] + far:
                    up_got_copy(u, origin).wait_recv()
                    total = total + up_got[u, origin].astype(f32)

                @pl.when(phase == 0)
                def _():
                    up_first[u] = total.astype(bf16)
                    uy_copy(u).start()

                @pl.when(phase == 1)
                def _():
                    up_second[u] = total.astype(bf16)

    def up_drain(phase, units):
        @pl.loop(0, units)
        def _(u):
            for k in range(R):
                @pl.when(jnp.logical_and(r < R - 1, k <= r))
                def _():
                    ux_copy(u, k, 1).wait_send()

                @pl.when(jnp.logical_and(r > 0, k >= r))
                def _():
                    ux_copy(u, k, 0).wait_send()

            for to in [sib] + far:
                up_copy(u, to).wait_send()
            for j in range(2, C, 2):
                mid_copy(u, lax.rem(sib + j, C)).wait_send()

            @pl.when(phase == 0)
            def _():
                uy_copy(u).wait_send()

    def down_form(phase, units):
        @pl.when(phase == 0)
        def _():
            @pl.loop(0, NB)
            def _(u):
                dx[u, c] = formed(src_t[u], gain_down[...], jnp.zeros((b, n), bf16))
                for to in far + [sib]:
                    dx_copy(u, to).start()

    def down_rest():
        @pl.loop(0, NB)
        def _(u):
            dy_copy(u).wait_recv()

        @pl.loop(1, T)
        def _(t):
            prev = dn_in[plan[t - 1, other, 1]]
            dx[t, c] = formed(src_t[plan[t, slab, 1]], gain_down[...], prev)
            for to in far + [sib]:
                dx_copy(t, to).start()

    def down_sweep(phase, units):
        down_form(phase, units)

        @pl.loop(0, units + R - 1)
        def _(i):
            @pl.when(i < units)
            def _():
                for origin in far:
                    dx_got_copy(i, origin).wait_recv()
                    pass_copy(i, origin).start()
                for origin in [sib] + [lax.rem(sib + j, C) for j in range(2, C, 2)]:
                    dx_got_copy(i, origin).wait_recv()

                @pl.loop(0, R)
                def _(k):
                    cols = pl.ds(pl.multiple_of(k * n, n), n)
                    total = jnp.dot(dx[i, 0], g[0:n, cols], preferred_element_type=f32)
                    for q in range(1, C):
                        total += jnp.dot(dx[i, q], g[q * n:(q + 1) * n, cols], preferred_element_type=f32)
                    dn_part[i, k] = total.astype(bf16)

            @pl.when(jnp.logical_and(phase == 1, i == 0))
            def _():
                down_rest()

            ur = i - r

            @pl.when(jnp.logical_and(r < R - 1, jnp.logical_and(ur >= 0, ur < units)))
            def _():
                for d in reversed(range(1, R)):
                    @pl.when(d > r)
                    def _():
                        @pl.when(r == 0)
                        def _():
                            dn_right[ur, d] = dn_part[ur, d]

                        @pl.when(r > 0)
                        def _():
                            dr_copy(ur, d).wait_recv()
                            dn_right[ur, d] = (dn_part[ur, d].astype(f32) + dn_from_left[ur, d].astype(f32)).astype(bf16)

                        dr_copy(ur, d).start()

            ul = i - (R - 1 - r)

            @pl.when(jnp.logical_and(r > 0, jnp.logical_and(ul >= 0, ul < units)))
            def _():
                for d in range(R - 1):
                    @pl.when(d < r)
                    def _():
                        @pl.when(r == R - 1)
                        def _():
                            dn_left[ul, d] = dn_part[ul, d]

                        @pl.when(r < R - 1)
                        def _():
                            dl_copy(ul, d).wait_recv()
                            dn_left[ul, d] = (dn_part[ul, d].astype(f32) + dn_from_right[ul, d].astype(f32)).astype(bf16)

                        dl_copy(ul, d).start()

            @pl.when(i >= R - 1)
            def _():
                u = i - (R - 1)

                def finish(total):
                    @pl.when(phase == 0)
                    def _():
                        dn_first[u] = total.astype(bf16)
                        dy_copy(u).start()

                    @pl.when(phase == 1)
                    def _():
                        dn_second[u] = total.astype(bf16)

                @pl.when(r > 0)
                def _():
                    dr_copy(u, r).wait_recv()

                @pl.when(r < R - 1)
                def _():
                    dl_copy(u, r).wait_recv()

                mine = dn_part[u, r].astype(f32)

                @pl.when(r == 0)
                def _():
                    finish(mine + dn_from_right[u, r].astype(f32))

                @pl.when(r == R - 1)
                def _():
                    finish(mine + dn_from_left[u, r].astype(f32))

                @pl.when(jnp.logical_and(r > 0, r < R - 1))
                def _():
                    finish(mine + dn_from_left[u, r].astype(f32) + dn_from_right[u, r].astype(f32))

    def down_drain(phase, units):
        @pl.loop(0, units)
        def _(u):
            for to in far + [sib]:
                dx_copy(u, to).wait_send()
            for origin in far:
                pass_copy(u, origin).wait_send()
            for d in range(R):
                @pl.when(d > r)
                def _():
                    dr_copy(u, d).wait_send()

                @pl.when(d < r)
                def _():
                    dl_copy(u, d).wait_send()

            @pl.when(phase == 0)
            def _():
                dy_copy(u).wait_send()

    @pl.when(slab == 0)
    def _():
        dx[0, c] = formed(src_t[plan[0, slab, 1]], gain_down[...], jnp.zeros((b, n), bf16))
        for to in far + [sib]:
            dx_copy(0, to).start()

    @pl.when(slab == 1)
    def _():
        ux[0, r] = formed(src[plan[0, slab, 0]], gain_up[...], jnp.zeros((n, b), bf16))
        own(0)

    @pl.loop(0, 2)
    def _(phase):
        units = jnp.where(phase == 0, NB, T)
        upward = lax.rem(phase + slab, 2) == 0

        @pl.when(upward)
        def _():
            up_sweep(phase, units)
            up_drain(phase, units)

        @pl.when(jnp.logical_not(upward))
        def _():
            down_sweep(phase, units)
            down_drain(phase, units)

    @pl.when(slab == 0)
    def _():
        up_out[...] = up_first[plan[T - 1, slab, 0]]
        down_out[...] = dn_second[T - 1]

    @pl.when(slab == 1)
    def _():
        up_out[...] = up_second[T - 1]
        down_out[...] = dn_first[plan[T - 1, slab, 1]]


def two_slabs(R, C, inverse, sources, coupling, plan):
    matrix = inverse[0].reshape(inverse.shape[1], -1)
    src = sources[0]
    NB, n, b = src.shape
    T = TICKS
    V = lambda *shape: pltpu.VMEM(shape, bf16)
    D = lambda *shape: pltpu.SemaphoreType.DMA(shape)
    vmem = pl.BlockSpec(memory_space=pltpu.VMEM)
    flops = 2 * matrix.size * b * (NB + T)
    up, down_t = pl.pallas_call(
        functools.partial(sweep_kernel, R, C, NB, T),
        out_shape=(jax.ShapeDtypeStruct((n, b), bf16), jax.ShapeDtypeStruct((b, n), bf16)),
        in_specs=[pl.BlockSpec(memory_space=pltpu.SMEM)] + [vmem] * 5,
        out_specs=(vmem, vmem),
        scratch_shapes=[
            V(T, R, n, b), V(T, C, n, b), V(T, C, n, b), V(T, C, n, b), V(NB, n, b), V(T, n, b), V(NB, n, b),
            V(T, C, b, n), V(T, R, b, n), V(T, R, b, n), V(T, R, b, n), V(T, R, b, n), V(T, R, b, n),
            V(NB, b, n), V(T, b, n), V(NB, b, n),
            D(T, R, 2), D(T, R), D(T, C), D(T, C), D(NB), D(NB),
            D(T, C), D(T, C), D(T, R), D(T, R), D(T, R), D(T, R), D(NB), D(NB),
            D(T, C), D(T, C), D(T, C),
        ],
        compiler_params=pltpu.CompilerParams(
            collective_id=0, has_side_effects=True, vmem_limit_bytes=56 * 1024 * 1024
        ),
        cost_estimate=pl.CostEstimate(flops=flops, bytes_accessed=2 * matrix.size, transcendentals=0),
    )(
        plan, matrix, src, jnp.swapaxes(src, 1, 2), coupling[0, 0][:, None], coupling[0, 1][None, :],
    )
    return up[None], down_t.T[None]


def solution(mesh):
    placed = (
        P("slab", "row", None, "col"),
        P("slab", None, ("row", "col"), None),
        P("slab", None, ("row", "col")),
        P(),
    )
    sizes = mesh.shape
    body = tick_by_tick
    if sizes["slab"] == 2 and sizes["row"] > 2 and sizes["col"] % 2 == 0:
        body = functools.partial(two_slabs, sizes["row"], sizes["col"])
    return jax.shard_map(
        body,
        mesh=mesh,
        in_specs=placed,
        out_specs=(P("slab", ("row", "col"), None), P("slab", ("row", "col"), None)),
        check_vma=False,
    )
```

```python
import functools

import jax
import jax.numpy as jnp
from jax import lax
from jax.experimental import pallas as pl
from jax.experimental.pallas import tpu as pltpu
from jax.sharding import PartitionSpec as P

TICKS = 6
MESH = pl.DeviceIdType.MESH
CHUNK = 128
f32 = jnp.float32
bf16 = jnp.bfloat16


def shifted(value, axis, steps):
    count = lax.axis_size(axis)
    leading, last = (max(0, -steps), min(count, count - steps))
    return lax.ppermute(value, axis, [(source, source + steps) for source in range(leading, last)])


def tick_by_tick(inverse, sources, coupling, plan):
    local_block = inverse[0]
    matrix = local_block.reshape(local_block.shape[0], -1)
    piece_rows, batch_width = sources.shape[2:]
    slab_index = lax.axis_index("slab")
    up_gain = coupling[0, 0][:, None]
    down_gain = coupling[0, 1][:, None]
    stored = sources[0]
    up_out = jnp.zeros((piece_rows, batch_width), bf16)
    down_out = jnp.zeros((piece_rows, batch_width), bf16)
    for tick in range(TICKS):
        up_recv, down_recv = up_out, down_out
        if tick:
            up_recv = shifted(up_out, "slab", 1)
            down_recv = shifted(down_out, "slab", -1)
        up_source = lax.dynamic_index_in_dim(stored, plan[tick, slab_index, 0], 0, keepdims=False)
        down_source = lax.dynamic_index_in_dim(stored, plan[tick, slab_index, 1], 0, keepdims=False)
        up_in = (up_source.astype(f32) + up_gain * up_recv.astype(f32)).astype(bf16)
        down_in = (down_source.astype(f32) + down_gain * down_recv.astype(f32)).astype(bf16)
        up_part = jnp.dot(matrix, lax.all_gather(up_in, "row", axis=0, tiled=True), preferred_element_type=f32)
        up_out = lax.psum_scatter(up_part.astype(bf16), "col", scatter_dimension=0, tiled=True)
        down_part = lax.dot_general(
            matrix,
            lax.all_gather(down_in, "col", axis=0, tiled=True),
            (((0,), (0,)), ((), ())),
            preferred_element_type=f32,
        )
        down_out = lax.psum_scatter(down_part.astype(bf16), "row", scatter_dimension=0, tiled=True)
    return (up_out[None], down_out[None])


def sweep_kernel(
    R, C, NB, T,
    plan, raw, src, coupling,
    up_out, down_out,
    ux, up_part, up_got, up_mid, up_first, up_second, up_in,
    dx, dn_part, dn_right, dn_left, dn_from_left, dn_from_right, dn_first, dn_second, dn_in,
    ux_s, ux_r, up_s, up_r, uy_s, uy_r,
    dx_s, dx_r, dr_s, dr_r, dl_s, dl_r, dy_s, dy_r,
    mid_s, mid_r, pass_s,
    g, src_t, gain_up, gain_down,
):
    slab, r, c = lax.axis_index("slab"), lax.axis_index("row"), lax.axis_index("col")
    other = 1 - slab
    n, b = src.shape[1], src.shape[2]
    sib = c + 1 - 2 * lax.rem(c, 2)
    far = [lax.rem(c + j, C) for j in range(2, C, 2)]

    gain_down[...] = coupling[1:2, :]
    gain_up[...] = jnp.broadcast_to(coupling[0:1, :], (b, n)).T
    for u in range(NB):
        src_t[u] = src[u].astype(f32).T.astype(bf16)

    barrier = pltpu.get_barrier_semaphore()
    for step in (1, R - 1):
        pl.semaphore_signal(barrier, inc=1, device_id={"row": lax.rem(r + step, R)}, device_id_type=MESH)
    for step in range(1, C):
        pl.semaphore_signal(barrier, inc=1, device_id={"col": lax.rem(c + step, C)}, device_id_type=MESH)
    pl.semaphore_signal(barrier, inc=1, device_id={"slab": other}, device_id_type=MESH)
    pl.semaphore_wait(barrier, 2 + (C - 1) + 1)

    def remote(source, target, send, recv, **where):
        return pltpu.make_async_remote_copy(
            src_ref=source, dst_ref=target, send_sem=send, recv_sem=recv, device_id=where, device_id_type=MESH
        )

    def ux_copy(u, k, way):
        to = jnp.minimum(r + 1, R - 1) if way else jnp.maximum(r - 1, 0)
        return remote(ux.at[u, k], ux.at[u, k], ux_s.at[u, k, way], ux_r.at[u, k], row=to)

    def up_copy(u, to):
        return remote(up_part.at[u, to], up_got.at[u, c], up_s.at[u, to], up_r.at[u, c], col=to)

    def up_got_copy(u, origin):
        return remote(up_part.at[u, origin], up_got.at[u, origin], up_s.at[u, origin], up_r.at[u, origin], col=origin)

    def mid_copy(u, dest):
        return remote(up_part.at[u, dest], up_mid.at[u, dest], mid_s.at[u, dest], mid_r.at[u, dest], col=sib)

    def uy_copy(u):
        return remote(up_first.at[u], up_in.at[u], uy_s.at[u], uy_r.at[u], slab=other)

    def dx_copy(u, to):
        return remote(dx.at[u, c], dx.at[u, c], dx_s.at[u, to], dx_r.at[u, c], col=to)

    def pass_copy(u, origin):
        return remote(dx.at[u, origin], dx.at[u, origin], pass_s.at[u, origin], dx_r.at[u, origin], col=sib)

    def dx_got_copy(u, origin):
        return remote(dx.at[u, origin], dx.at[u, origin], dx_s.at[u, origin], dx_r.at[u, origin], col=origin)

    def dr_copy(u, d):
        return remote(dn_right.at[u, d], dn_from_left.at[u, d], dr_s.at[u, d], dr_r.at[u, d], row=jnp.minimum(r + 1, R - 1))

    def dl_copy(u, d):
        return remote(dn_left.at[u, d], dn_from_right.at[u, d], dl_s.at[u, d], dl_r.at[u, d], row=jnp.maximum(r - 1, 0))

    def dy_copy(u):
        return remote(dn_first.at[u], dn_in.at[u], dy_s.at[u], dy_r.at[u], slab=other)

    def formed(source, gain, prev):
        return (source.astype(f32) + gain * prev.astype(f32)).astype(bf16)

    def up_form(phase, units):
        @pl.when(phase == 1)
        def _():
            @pl.loop(0, NB)
            def _(u):
                uy_copy(u).wait_recv()

            @pl.loop(1, T)
            def _(t):
                prev = up_in[plan[t - 1, other, 0]]
                ux[t, r] = formed(src[plan[t, slab, 0]], gain_up[...], prev)

    def own(u):
        @pl.when(r < R - 1)
        def _():
            ux_copy(u, r, 1).start()

        @pl.when(r > 0)
        def _():
            ux_copy(u, r, 0).start()

    def up_sweep(phase, units):
        up_form(phase, units)

        @pl.loop(0, units + R - 1)
        def _(i):
            @pl.when(i + 1 < units)
            def _():
                own(i + 1)

            for d in reversed(range(1, R)):
                u = i - (d - 1)

                @pl.when(jnp.logical_and(u >= 0, u < units))
                def _():
                    @pl.when(r - d >= 0)
                    def _():
                        ux_copy(u, r - d, 1).wait_recv()

                        @pl.when(r < R - 1)
                        def _():
                            ux_copy(u, r - d, 1).start()

                    @pl.when(r + d < R)
                    def _():
                        ux_copy(u, r + d, 0).wait_recv()

                        @pl.when(r > 0)
                        def _():
                            ux_copy(u, r + d, 0).start()

            um = i - (R - 2)

            @pl.when(jnp.logical_and(um >= 0, um < units))
            def _():
                @pl.loop(1, C // 2 + 1)
                def _(j):
                    to = lax.rem(sib + 2 * j, C)
                    rows = pl.ds(pl.multiple_of(to * n, n), n)
                    x = ux[um].reshape(R * n, b)
                    up_part[um, to] = jnp.dot(g[rows, :], x, preferred_element_type=f32).astype(bf16)

                    @pl.when(j < C // 2)
                    def _():
                        mid_copy(um, to).start()

                    @pl.when(j == C // 2)
                    def _():
                        up_copy(um, sib).start()

                @pl.loop(1, C // 2 + 1)
                def _(j):
                    to = lax.rem(c + 2 * j, C)
                    rows = pl.ds(pl.multiple_of(to * n, n), n)
                    x = ux[um].reshape(R * n, b)
                    up_part[um, to] = jnp.dot(g[rows, :], x, preferred_element_type=f32).astype(bf16)

                    @pl.when(j < C // 2)
                    def _():
                        mid_copy(um, to).wait_recv()
                        up_part[um, to] = (up_part[um, to].astype(f32) + up_mid[um, to].astype(f32)).astype(bf16)
                        up_copy(um, to).start()

            @pl.when(i >= R - 1)
            def _():
                u = i - (R - 1)
                total = up_part[u, c].astype(f32)
                for origin in [sib] + far:
                    up_got_copy(u, origin).wait_recv()
                    total = total + up_got[u, origin].astype(f32)

                @pl.when(phase == 0)
                def _():
                    up_first[u] = total.astype(bf16)
                    uy_copy(u).start()

                @pl.when(phase == 1)
                def _():
                    up_second[u] = total.astype(bf16)

    def up_drain(phase, units):
        @pl.loop(0, units)
        def _(u):
            for k in range(R):
                @pl.when(jnp.logical_and(r < R - 1, k <= r))
                def _():
                    ux_copy(u, k, 1).wait_send()

                @pl.when(jnp.logical_and(r > 0, k >= r))
                def _():
                    ux_copy(u, k, 0).wait_send()

            for to in [sib] + far:
                up_copy(u, to).wait_send()
            for j in range(2, C, 2):
                mid_copy(u, lax.rem(sib + j, C)).wait_send()

            @pl.when(phase == 0)
            def _():
                uy_copy(u).wait_send()

    def down_rest():
        @pl.loop(0, NB)
        def _(u):
            dy_copy(u).wait_recv()

        @pl.loop(1, T)
        def _(t):
            prev = dn_in[plan[t - 1, other, 1]]
            dx[t, c] = formed(src_t[plan[t, slab, 1]], gain_down[...], prev)
            for to in far + [sib]:
                dx_copy(t, to).start()

    def down_sweep(phase, units):
        @pl.loop(0, units + R - 1)
        def _(i):
            @pl.when(i < units)
            def _():
                for origin in far:
                    dx_got_copy(i, origin).wait_recv()
                    pass_copy(i, origin).start()
                for origin in [sib] + [lax.rem(sib + j, C) for j in range(2, C, 2)]:
                    dx_got_copy(i, origin).wait_recv()

                @pl.loop(0, R)
                def _(k):
                    cols = pl.ds(pl.multiple_of(k * n, n), n)
                    total = jnp.dot(dx[i, 0], g[0:n, cols], preferred_element_type=f32)
                    for q in range(1, C):
                        total += jnp.dot(dx[i, q], g[q * n:(q + 1) * n, cols], preferred_element_type=f32)
                    dn_part[i, k] = total.astype(bf16)

            @pl.when(jnp.logical_and(phase == 1, i == 0))
            def _():
                down_rest()

            ur = i - r

            @pl.when(jnp.logical_and(r < R - 1, jnp.logical_and(ur >= 0, ur < units)))
            def _():
                for d in reversed(range(1, R)):
                    @pl.when(d > r)
                    def _():
                        @pl.when(r == 0)
                        def _():
                            dn_right[ur, d] = dn_part[ur, d]

                        @pl.when(r > 0)
                        def _():
                            dr_copy(ur, d).wait_recv()
                            dn_right[ur, d] = (dn_part[ur, d].astype(f32) + dn_from_left[ur, d].astype(f32)).astype(bf16)

                        dr_copy(ur, d).start()

            ul = i - (R - 1 - r)

            @pl.when(jnp.logical_and(r > 0, jnp.logical_and(ul >= 0, ul < units)))
            def _():
                for d in range(R - 1):
                    @pl.when(d < r)
                    def _():
                        @pl.when(r == R - 1)
                        def _():
                            dn_left[ul, d] = dn_part[ul, d]

                        @pl.when(r < R - 1)
                        def _():
                            dl_copy(ul, d).wait_recv()
                            dn_left[ul, d] = (dn_part[ul, d].astype(f32) + dn_from_right[ul, d].astype(f32)).astype(bf16)

                        dl_copy(ul, d).start()

            @pl.when(i >= R - 1)
            def _():
                u = i - (R - 1)

                def finish(total):
                    @pl.when(phase == 0)
                    def _():
                        dn_first[u] = total.astype(bf16)
                        dy_copy(u).start()

                    @pl.when(phase == 1)
                    def _():
                        dn_second[u] = total.astype(bf16)

                @pl.when(r > 0)
                def _():
                    dr_copy(u, r).wait_recv()

                @pl.when(r < R - 1)
                def _():
                    dl_copy(u, r).wait_recv()

                mine = dn_part[u, r].astype(f32)

                @pl.when(r == 0)
                def _():
                    finish(mine + dn_from_right[u, r].astype(f32))

                @pl.when(r == R - 1)
                def _():
                    finish(mine + dn_from_left[u, r].astype(f32))

                @pl.when(jnp.logical_and(r > 0, r < R - 1))
                def _():
                    finish(mine + dn_from_left[u, r].astype(f32) + dn_from_right[u, r].astype(f32))

    def down_drain(phase, units):
        @pl.loop(0, units)
        def _(u):
            for to in far + [sib]:
                dx_copy(u, to).wait_send()
            for origin in far:
                pass_copy(u, origin).wait_send()
            for d in range(R):
                @pl.when(d > r)
                def _():
                    dr_copy(u, d).wait_send()

                @pl.when(d < r)
                def _():
                    dl_copy(u, d).wait_send()

            @pl.when(phase == 0)
            def _():
                dy_copy(u).wait_send()

    @pl.when(slab == 0)
    def _():
        dx[0, c] = formed(src_t[plan[0, slab, 1]], gain_down[...], jnp.zeros((b, n), bf16))
        for to in far + [sib]:
            dx_copy(0, to).start()

    @pl.when(slab == 1)
    def _():
        ux[0, r] = formed(src[plan[0, slab, 0]], gain_up[...], jnp.zeros((n, b), bf16))
        own(0)

    @pl.when(slab == 0)
    def _():
        @pl.loop(0, NB)
        def _(u):
            ux[u, r] = formed(src[u], gain_up[...], jnp.zeros((n, b), bf16))

        own(0)

    @pl.when(slab == 1)
    def _():
        @pl.loop(0, NB)
        def _(u):
            dx[u, c] = formed(src_t[u], gain_down[...], jnp.zeros((b, n), bf16))
            for to in far + [sib]:
                dx_copy(u, to).start()

    @pl.loop(0, raw.shape[0] // CHUNK)
    def _(q):
        rows = pl.ds(pl.multiple_of(q * CHUNK, CHUNK), CHUNK)
        g[rows, :] = raw[rows].reshape(CHUNK, g.shape[1])

    @pl.loop(0, 2)
    def _(phase):
        units = jnp.where(phase == 0, NB, T)
        upward = lax.rem(phase + slab, 2) == 0

        @pl.when(upward)
        def _():
            up_sweep(phase, units)
            up_drain(phase, units)

        @pl.when(jnp.logical_not(upward))
        def _():
            down_sweep(phase, units)
            down_drain(phase, units)

    @pl.when(slab == 0)
    def _():
        up_out[...] = up_first[plan[T - 1, slab, 0]]
        down_out[...] = dn_second[T - 1]

    @pl.when(slab == 1)
    def _():
        up_out[...] = up_second[T - 1]
        down_out[...] = dn_first[plan[T - 1, slab, 1]]


def two_slabs(R, C, inverse, sources, coupling, plan):
    raw = inverse[0]
    src = sources[0]
    NB, n, b = src.shape
    T = TICKS
    V = lambda *shape: pltpu.VMEM(shape, bf16)
    D = lambda *shape: pltpu.SemaphoreType.DMA(shape)
    vmem = pl.BlockSpec(memory_space=pltpu.VMEM)
    flops = 2 * raw.size * b * (NB + T)
    up, down_t = pl.pallas_call(
        functools.partial(sweep_kernel, R, C, NB, T),
        out_shape=(jax.ShapeDtypeStruct((n, b), bf16), jax.ShapeDtypeStruct((b, n), bf16)),
        in_specs=[pl.BlockSpec(memory_space=pltpu.SMEM)] + [vmem] * 3,
        out_specs=(vmem, vmem),
        scratch_shapes=[
            V(T, R, n, b), V(T, C, n, b), V(T, C, n, b), V(T, C, n, b), V(NB, n, b), V(T, n, b), V(NB, n, b),
            V(T, C, b, n), V(T, R, b, n), V(T, R, b, n), V(T, R, b, n), V(T, R, b, n), V(T, R, b, n),
            V(NB, b, n), V(T, b, n), V(NB, b, n),
            D(T, R, 2), D(T, R), D(T, C), D(T, C), D(NB), D(NB),
            D(T, C), D(T, C), D(T, R), D(T, R), D(T, R), D(T, R), D(NB), D(NB),
            D(T, C), D(T, C), D(T, C),
            V(raw.shape[0], raw.shape[1] * raw.shape[2]), V(NB, b, n),
            pltpu.VMEM((n, b), f32), pltpu.VMEM((1, n), f32),
        ],
        compiler_params=pltpu.CompilerParams(
            collective_id=0, has_side_effects=True, vmem_limit_bytes=56 * 1024 * 1024
        ),
        cost_estimate=pl.CostEstimate(flops=flops, bytes_accessed=2 * raw.size, transcendentals=0),
    )(
        plan, raw, src, coupling[0],
    )
    return up[None], down_t.T[None]


def solution(mesh):
    placed = (
        P("slab", "row", None, "col"),
        P("slab", None, ("row", "col"), None),
        P("slab", None, ("row", "col")),
        P(),
    )
    sizes = mesh.shape
    body = tick_by_tick
    if sizes["slab"] == 2 and sizes["row"] > 2 and sizes["col"] % 2 == 0:
        body = functools.partial(two_slabs, sizes["row"], sizes["col"])
    return jax.shard_map(
        body,
        mesh=mesh,
        in_specs=placed,
        out_specs=(P("slab", ("row", "col"), None), P("slab", ("row", "col"), None)),
        check_vma=False,
    )
```

```python
import functools

import jax
import jax.numpy as jnp
from jax import lax
from jax.experimental import pallas as pl
from jax.experimental.pallas import tpu as pltpu
from jax.sharding import PartitionSpec as P

TICKS = 6
MESH = pl.DeviceIdType.MESH
CHUNK = 128
f32 = jnp.float32
bf16 = jnp.bfloat16


def shifted(value, axis, steps):
    count = lax.axis_size(axis)
    leading, last = (max(0, -steps), min(count, count - steps))
    return lax.ppermute(value, axis, [(source, source + steps) for source in range(leading, last)])


def tick_by_tick(inverse, sources, coupling, plan):
    local_block = inverse[0]
    matrix = local_block.reshape(local_block.shape[0], -1)
    piece_rows, batch_width = sources.shape[2:]
    slab_index = lax.axis_index("slab")
    up_gain = coupling[0, 0][:, None]
    down_gain = coupling[0, 1][:, None]
    stored = sources[0]
    up_out = jnp.zeros((piece_rows, batch_width), bf16)
    down_out = jnp.zeros((piece_rows, batch_width), bf16)
    for tick in range(TICKS):
        up_recv, down_recv = up_out, down_out
        if tick:
            up_recv = shifted(up_out, "slab", 1)
            down_recv = shifted(down_out, "slab", -1)
        up_source = lax.dynamic_index_in_dim(stored, plan[tick, slab_index, 0], 0, keepdims=False)
        down_source = lax.dynamic_index_in_dim(stored, plan[tick, slab_index, 1], 0, keepdims=False)
        up_in = (up_source.astype(f32) + up_gain * up_recv.astype(f32)).astype(bf16)
        down_in = (down_source.astype(f32) + down_gain * down_recv.astype(f32)).astype(bf16)
        up_part = jnp.dot(matrix, lax.all_gather(up_in, "row", axis=0, tiled=True), preferred_element_type=f32)
        up_out = lax.psum_scatter(up_part.astype(bf16), "col", scatter_dimension=0, tiled=True)
        down_part = lax.dot_general(
            matrix,
            lax.all_gather(down_in, "col", axis=0, tiled=True),
            (((0,), (0,)), ((), ())),
            preferred_element_type=f32,
        )
        down_out = lax.psum_scatter(down_part.astype(bf16), "row", scatter_dimension=0, tiled=True)
    return (up_out[None], down_out[None])


def sweep_kernel(
    R, C, NB, T,
    plan, raw, src, coupling,
    up_out, down_out,
    ux, up_part, up_got, up_mid, up_first, up_second, up_in,
    dx, dn_part, dn_right, dn_left, dn_from_left, dn_from_right, dn_first, dn_second, dn_in,
    ux_s, ux_r, up_s, up_r, uy_s, uy_r,
    dx_s, dx_r, dr_s, dr_r, dl_s, dl_r, dy_s, dy_r,
    mid_s, mid_r, pass_s,
    g, src_t, gain_up, gain_down,
):
    slab, r, c = lax.axis_index("slab"), lax.axis_index("row"), lax.axis_index("col")
    other = 1 - slab
    n, b = src.shape[1], src.shape[2]
    sib = c + 1 - 2 * lax.rem(c, 2)
    far = [lax.rem(c + j, C) for j in range(2, C, 2)]

    gain_down[...] = coupling[1:2, :]
    gain_up[...] = jnp.broadcast_to(coupling[0:1, :], (b, n)).T
    for u in range(NB):
        src_t[u] = src[u].astype(f32).T.astype(bf16)

    barrier = pltpu.get_barrier_semaphore()
    for step in (1, R - 1):
        pl.semaphore_signal(barrier, inc=1, device_id={"row": lax.rem(r + step, R)}, device_id_type=MESH)
    for step in range(1, C):
        pl.semaphore_signal(barrier, inc=1, device_id={"col": lax.rem(c + step, C)}, device_id_type=MESH)
    pl.semaphore_signal(barrier, inc=1, device_id={"slab": other}, device_id_type=MESH)
    pl.semaphore_wait(barrier, 2 + (C - 1) + 1)

    def remote(source, target, send, recv, **where):
        return pltpu.make_async_remote_copy(
            src_ref=source, dst_ref=target, send_sem=send, recv_sem=recv, device_id=where, device_id_type=MESH
        )

    def ux_copy(u, k, way):
        to = jnp.minimum(r + 1, R - 1) if way else jnp.maximum(r - 1, 0)
        return remote(ux.at[u, k], ux.at[u, k], ux_s.at[u, k, way], ux_r.at[u, k], row=to)

    def up_copy(u, to):
        return remote(up_part.at[u, to], up_got.at[u, c], up_s.at[u, to], up_r.at[u, c], col=to)

    def up_got_copy(u, origin):
        return remote(up_part.at[u, origin], up_got.at[u, origin], up_s.at[u, origin], up_r.at[u, origin], col=origin)

    def mid_copy(u, dest):
        return remote(up_part.at[u, dest], up_mid.at[u, dest], mid_s.at[u, dest], mid_r.at[u, dest], col=sib)

    def uy_copy(u):
        return remote(up_first.at[u], up_in.at[u], uy_s.at[u], uy_r.at[u], slab=other)

    def dx_copy(u, to):
        return remote(dx.at[u, c], dx.at[u, c], dx_s.at[u, to], dx_r.at[u, c], col=to)

    def pass_copy(u, origin):
        return remote(dx.at[u, origin], dx.at[u, origin], pass_s.at[u, origin], dx_r.at[u, origin], col=sib)

    def dx_got_copy(u, origin):
        return remote(dx.at[u, origin], dx.at[u, origin], dx_s.at[u, origin], dx_r.at[u, origin], col=origin)

    def dr_copy(u, d):
        return remote(dn_right.at[u, d], dn_from_left.at[u, d], dr_s.at[u, d], dr_r.at[u, d], row=jnp.minimum(r + 1, R - 1))

    def dl_copy(u, d):
        return remote(dn_left.at[u, d], dn_from_right.at[u, d], dl_s.at[u, d], dl_r.at[u, d], row=jnp.maximum(r - 1, 0))

    def dy_copy(u):
        return remote(dn_first.at[u], dn_in.at[u], dy_s.at[u], dy_r.at[u], slab=other)

    def formed(source, gain, prev):
        return (source.astype(f32) + gain * prev.astype(f32)).astype(bf16)

    def up_form(phase, units):
        @pl.when(phase == 1)
        def _():
            @pl.loop(0, NB)
            def _(u):
                uy_copy(u).wait_recv()

            @pl.loop(1, T)
            def _(t):
                prev = up_in[plan[t - 1, other, 0]]
                ux[t, r] = formed(src[plan[t, slab, 0]], gain_up[...], prev)

    def own(u):
        @pl.when(r < R - 1)
        def _():
            ux_copy(u, r, 1).start()

        @pl.when(r > 0)
        def _():
            ux_copy(u, r, 0).start()

    def up_sweep(phase, units):
        up_form(phase, units)

        @pl.when(phase == 1)
        def _():
            own(1)

        @pl.loop(0, units + R - 1)
        def _(i):
            @pl.when(i + 2 < units)
            def _():
                own(i + 2)

            for d in reversed(range(1, R)):
                u = i - (d - 1)

                @pl.when(jnp.logical_and(u >= 0, u < units))
                def _():
                    @pl.when(r - d >= 0)
                    def _():
                        ux_copy(u, r - d, 1).wait_recv()

                        @pl.when(r < R - 1)
                        def _():
                            ux_copy(u, r - d, 1).start()

                    @pl.when(r + d < R)
                    def _():
                        ux_copy(u, r + d, 0).wait_recv()

                        @pl.when(r > 0)
                        def _():
                            ux_copy(u, r + d, 0).start()

            um = i - (R - 2)

            @pl.when(jnp.logical_and(um >= 0, um < units))
            def _():
                @pl.loop(1, C // 2 + 1)
                def _(j):
                    to = lax.rem(sib + 2 * j, C)
                    rows = pl.ds(pl.multiple_of(to * n, n), n)
                    x = ux[um].reshape(R * n, b)
                    up_part[um, to] = jnp.dot(g[rows, :], x, preferred_element_type=f32).astype(bf16)

                    @pl.when(j < C // 2)
                    def _():
                        mid_copy(um, to).start()

                    @pl.when(j == C // 2)
                    def _():
                        up_copy(um, sib).start()

                @pl.loop(1, C // 2 + 1)
                def _(j):
                    to = lax.rem(c + 2 * j, C)
                    rows = pl.ds(pl.multiple_of(to * n, n), n)
                    x = ux[um].reshape(R * n, b)
                    up_part[um, to] = jnp.dot(g[rows, :], x, preferred_element_type=f32).astype(bf16)

                    @pl.when(j < C // 2)
                    def _():
                        mid_copy(um, to).wait_recv()
                        up_part[um, to] = (up_part[um, to].astype(f32) + up_mid[um, to].astype(f32)).astype(bf16)
                        up_copy(um, to).start()

            @pl.when(i >= R - 1)
            def _():
                u = i - (R - 1)
                total = up_part[u, c].astype(f32)
                for origin in [sib] + far:
                    up_got_copy(u, origin).wait_recv()
                    total = total + up_got[u, origin].astype(f32)

                @pl.when(phase == 0)
                def _():
                    up_first[u] = total.astype(bf16)
                    uy_copy(u).start()

                @pl.when(phase == 1)
                def _():
                    up_second[u] = total.astype(bf16)

    def up_drain(phase, units):
        @pl.loop(0, units)
        def _(u):
            for k in range(R):
                @pl.when(jnp.logical_and(r < R - 1, k <= r))
                def _():
                    ux_copy(u, k, 1).wait_send()

                @pl.when(jnp.logical_and(r > 0, k >= r))
                def _():
                    ux_copy(u, k, 0).wait_send()

            for to in [sib] + far:
                up_copy(u, to).wait_send()
            for j in range(2, C, 2):
                mid_copy(u, lax.rem(sib + j, C)).wait_send()

            if phase == 0:
                uy_copy(u).wait_send()

    def down_rest():
        @pl.loop(0, NB)
        def _(u):
            dy_copy(u).wait_recv()

        @pl.loop(1, T)
        def _(t):
            prev = dn_in[plan[t - 1, other, 1]]
            dx[t, c] = formed(src_t[plan[t, slab, 1]], gain_down[...], prev)
            for to in far + [sib]:
                dx_copy(t, to).start()

    def down_sweep(phase, units):
        @pl.loop(0, units + R - 1)
        def _(i):
            @pl.when(i < units)
            def _():
                for origin in far:
                    dx_got_copy(i, origin).wait_recv()
                    pass_copy(i, origin).start()
                for origin in [sib] + [lax.rem(sib + j, C) for j in range(2, C, 2)]:
                    dx_got_copy(i, origin).wait_recv()

                @pl.loop(0, R)
                def _(k):
                    cols = pl.ds(pl.multiple_of(k * n, n), n)
                    total = jnp.dot(dx[i, 0], g[0:n, cols], preferred_element_type=f32)
                    for q in range(1, C):
                        total += jnp.dot(dx[i, q], g[q * n:(q + 1) * n, cols], preferred_element_type=f32)
                    dn_part[i, k] = total.astype(bf16)

            ur = i - r

            @pl.when(jnp.logical_and(r < R - 1, jnp.logical_and(ur >= 0, ur < units)))
            def _():
                for d in reversed(range(1, R)):
                    @pl.when(d > r)
                    def _():
                        @pl.when(r == 0)
                        def _():
                            dn_right[ur, d] = dn_part[ur, d]

                        @pl.when(r > 0)
                        def _():
                            dr_copy(ur, d).wait_recv()
                            dn_right[ur, d] = (dn_part[ur, d].astype(f32) + dn_from_left[ur, d].astype(f32)).astype(bf16)

                        dr_copy(ur, d).start()

            ul = i - (R - 1 - r)

            @pl.when(jnp.logical_and(r > 0, jnp.logical_and(ul >= 0, ul < units)))
            def _():
                for d in range(R - 1):
                    @pl.when(d < r)
                    def _():
                        @pl.when(r == R - 1)
                        def _():
                            dn_left[ul, d] = dn_part[ul, d]

                        @pl.when(r < R - 1)
                        def _():
                            dl_copy(ul, d).wait_recv()
                            dn_left[ul, d] = (dn_part[ul, d].astype(f32) + dn_from_right[ul, d].astype(f32)).astype(bf16)

                        dl_copy(ul, d).start()

            @pl.when(i >= R - 1)
            def _():
                u = i - (R - 1)

                def finish(total):
                    @pl.when(phase == 0)
                    def _():
                        dn_first[u] = total.astype(bf16)
                        dy_copy(u).start()

                    @pl.when(phase == 1)
                    def _():
                        dn_second[u] = total.astype(bf16)

                @pl.when(r > 0)
                def _():
                    dr_copy(u, r).wait_recv()

                @pl.when(r < R - 1)
                def _():
                    dl_copy(u, r).wait_recv()

                mine = dn_part[u, r].astype(f32)

                @pl.when(r == 0)
                def _():
                    finish(mine + dn_from_right[u, r].astype(f32))

                @pl.when(r == R - 1)
                def _():
                    finish(mine + dn_from_left[u, r].astype(f32))

                @pl.when(jnp.logical_and(r > 0, r < R - 1))
                def _():
                    finish(mine + dn_from_left[u, r].astype(f32) + dn_from_right[u, r].astype(f32))

            @pl.when(jnp.logical_and(phase == 1, i == 0))
            def _():
                down_rest()

    def down_drain(phase, units):
        @pl.loop(0, units)
        def _(u):
            for to in far + [sib]:
                dx_copy(u, to).wait_send()
            for origin in far:
                pass_copy(u, origin).wait_send()
            for d in range(R):
                @pl.when(d > r)
                def _():
                    dr_copy(u, d).wait_send()

                @pl.when(d < r)
                def _():
                    dl_copy(u, d).wait_send()

            if phase == 0:
                dy_copy(u).wait_send()

    @pl.when(slab == 0)
    def _():
        dx[0, c] = formed(src_t[plan[0, slab, 1]], gain_down[...], jnp.zeros((b, n), bf16))
        for to in far + [sib]:
            dx_copy(0, to).start()

    @pl.when(slab == 1)
    def _():
        ux[0, r] = formed(src[plan[0, slab, 0]], gain_up[...], jnp.zeros((n, b), bf16))
        own(0)

    @pl.when(slab == 0)
    def _():
        @pl.loop(0, NB)
        def _(u):
            ux[u, r] = formed(src[u], gain_up[...], jnp.zeros((n, b), bf16))

        own(0)
        own(1)

    @pl.when(slab == 1)
    def _():
        @pl.loop(0, NB)
        def _(u):
            dx[u, c] = formed(src_t[u], gain_down[...], jnp.zeros((b, n), bf16))
            for to in far + [sib]:
                dx_copy(u, to).start()

    @pl.loop(0, raw.shape[0] // CHUNK)
    def _(q):
        rows = pl.ds(pl.multiple_of(q * CHUNK, CHUNK), CHUNK)
        g[rows, :] = raw[rows].reshape(CHUNK, g.shape[1])

    @pl.loop(0, 2)
    def _(phase):
        units = jnp.where(phase == 0, NB, T)
        upward = lax.rem(phase + slab, 2) == 0

        @pl.when(upward)
        def _():
            up_sweep(phase, units)

        @pl.when(jnp.logical_not(upward))
        def _():
            down_sweep(phase, units)

    @pl.when(slab == 0)
    def _():
        up_drain(0, NB)
        down_drain(1, T)
        up_out[...] = up_first[plan[T - 1, slab, 0]]
        down_out[...] = dn_second[T - 1]

    @pl.when(slab == 1)
    def _():
        down_drain(0, NB)
        up_drain(1, T)
        up_out[...] = up_second[T - 1]
        down_out[...] = dn_first[plan[T - 1, slab, 1]]


def two_slabs(R, C, inverse, sources, coupling, plan):
    raw = inverse[0]
    src = sources[0]
    NB, n, b = src.shape
    T = TICKS
    V = lambda *shape: pltpu.VMEM(shape, bf16)
    D = lambda *shape: pltpu.SemaphoreType.DMA(shape)
    vmem = pl.BlockSpec(memory_space=pltpu.VMEM)
    flops = 2 * raw.size * b * (NB + T)
    up, down_t = pl.pallas_call(
        functools.partial(sweep_kernel, R, C, NB, T),
        out_shape=(jax.ShapeDtypeStruct((n, b), bf16), jax.ShapeDtypeStruct((b, n), bf16)),
        in_specs=[pl.BlockSpec(memory_space=pltpu.SMEM)] + [vmem] * 3,
        out_specs=(vmem, vmem),
        scratch_shapes=[
            V(T, R, n, b), V(T, C, n, b), V(T, C, n, b), V(T, C, n, b), V(NB, n, b), V(T, n, b), V(NB, n, b),
            V(T, C, b, n), V(T, R, b, n), V(T, R, b, n), V(T, R, b, n), V(T, R, b, n), V(T, R, b, n),
            V(NB, b, n), V(T, b, n), V(NB, b, n),
            D(T, R, 2), D(T, R), D(T, C), D(T, C), D(NB), D(NB),
            D(T, C), D(T, C), D(T, R), D(T, R), D(T, R), D(T, R), D(NB), D(NB),
            D(T, C), D(T, C), D(T, C),
            V(raw.shape[0], raw.shape[1] * raw.shape[2]), V(NB, b, n),
            pltpu.VMEM((n, b), f32), pltpu.VMEM((1, n), f32),
        ],
        compiler_params=pltpu.CompilerParams(
            collective_id=0, has_side_effects=True, vmem_limit_bytes=56 * 1024 * 1024
        ),
        cost_estimate=pl.CostEstimate(flops=flops, bytes_accessed=2 * raw.size, transcendentals=0),
    )(
        plan, raw, src, coupling[0],
    )
    return up[None], down_t.T[None]


def solution(mesh):
    placed = (
        P("slab", "row", None, "col"),
        P("slab", None, ("row", "col"), None),
        P("slab", None, ("row", "col")),
        P(),
    )
    sizes = mesh.shape
    body = tick_by_tick
    if sizes["slab"] == 2 and sizes["row"] > 2 and sizes["col"] % 2 == 0:
        body = functools.partial(two_slabs, sizes["row"], sizes["col"])
    return jax.shard_map(
        body,
        mesh=mesh,
        in_specs=placed,
        out_specs=(P("slab", ("row", "col"), None), P("slab", ("row", "col"), None)),
        check_vma=False,
    )
```
